32 devices in a mesh: row: 8 (over y, x, core), col: 4 (over z).
Axes of the slice: x: 2, y: 2, z: 4, core: 2. Of those that a mesh axis runs over, the one named last changes fastest.
Arguments:
- covariance: float32 [2, 8, 512, 4, 4, 512], P(None, 'row', None, None, 'col'), as said below
- keep: int32 [2, 8, 4, 4], P(None, 'row', None, 'col'), may hold values from 0 to 1, as said below
Outputs:
- factor: float32 [2, 8, 512, 4, 4, 512], P(None, 'row', None, None, 'col')
The draws below stay inside these ranges and needn't reach their ends.
Inputs may be any that keep to these rules, and one draw needn't show every extreme that they name: covariance is symmetric and positive definite. keep is 1 for every tile pair whose row and column tiles lie in the same diagonal super-tile of 4 tiles (i // 4 == j // 4).
All inputs are finite; a program needn't handle non-finite values.
Results may differ from the reference program's by a relative error of at most 0.0001.
Values sent between devices are 32-bit elements; how exact they have to be, the bound alone decides.
A program may use at most 128 MiB of HBM per device.

```python
import math
import jax
import jax.numpy as jnp
from jax import lax

B = 512
MT = 2
SUPER = 4
NTC = 4
N_ROW = 8
N_COL = 4


def draw_covariance(key, part):
    order = MT * N_ROW * B
    reach = 2.0 * B
    first, second, third = jax.random.split(jax.random.fold_in(key, 11), 3)
    across = jax.random.uniform(first, (order,), jnp.float32) * reach
    along = jnp.arange(order).astype(jnp.float32)
    delta_x = along[:, None] - along[None, :]
    delta_y = across[:, None] - across[None, :]
    scaled = jnp.sqrt(delta_x * delta_x + delta_y * delta_y) * (math.sqrt(3.0) / reach)
    amplitude = 14.0 * math.sqrt(order / B)
    noise = jax.random.normal(second, (order, order), jnp.float32)
    matern = amplitude * (1.0 + scaled) * jnp.exp(-scaled)
    symmetric = (noise + noise.T) * (1.0 / math.sqrt(2.0))
    diagonal = math.sqrt(order) * (3.0 + jax.random.uniform(third, (order,), jnp.float32))
    full = (matern + symmetric + jnp.diag(diagonal)) * (1.0 / math.sqrt(order))
    return full.astype(jnp.float32).reshape(MT, N_ROW, B, MT * N_ROW // N_COL, N_COL, B)


def draw_keep(key, part):
    tile_count = MT * N_ROW
    coins = jax.random.randint(jax.random.fold_in(key, 23), (tile_count, tile_count), 0, 2)
    ids = jnp.arange(tile_count)
    same = ids[:, None] // SUPER == ids[None, :] // SUPER
    kept = jnp.where(same, 1, coins).astype(jnp.int32)
    return kept.reshape(MT, N_ROW, MT * N_ROW // N_COL, N_COL)


def setup_inputs(seed: int = 0) -> dict:
    arg_keys = jax.random.split(jax.random.key(seed), 3)
    return {
        "covariance": draw_covariance(jax.random.fold_in(arg_keys[2], 71), 0),
        "keep": draw_keep(jax.random.fold_in(arg_keys[2], 71), 0),
    }


def solve_rows(factor, column):
    count = column.shape[0]
    width = column.shape[1]
    stacked = jnp.transpose(column, (2, 0, 1)).reshape(width, count * width)
    solved = jax.scipy.linalg.solve_triangular(factor, stacked, lower=True)
    return jnp.transpose(solved.reshape(width, count, width), (1, 2, 0))

def reference(covariance, keep):
    tile_count = MT * N_ROW
    tiles = covariance.reshape(tile_count, B, tile_count, B)
    ids = jnp.arange(tile_count)
    live = (keep.reshape(tile_count, tile_count) > 0) & (ids[:, None] >= ids[None, :])
    tiles = jnp.where(live[:, None, :, None], tiles, jnp.float32(0.0))
    for step in range(2):
        factor = jnp.linalg.cholesky(tiles[step, :, step, :])
        solved = solve_rows(factor, tiles[:, :, step, :])
        panel = jnp.where(ids[:, None, None] > step, solved, jnp.where(ids[:, None, None] == step, factor[None], jnp.float32(0.0)))
        product = jnp.einsum('irb,jsb->irjs', panel, panel, precision=lax.Precision.HIGHEST)
        active = live & (ids > step)[:, None] & (ids > step)[None, :]
        tiles = jnp.where(active[:, None, :, None], tiles - product, tiles)
        tiles = jnp.where((ids == step)[None, None, :, None], panel[:, :, None, :], tiles)
    return tiles.reshape(MT, N_ROW, B, NTC, N_COL, B)
```

```python
import functools

import jax
import jax.numpy as jnp
from jax import lax
from jax.experimental import pallas as pl
from jax.experimental.pallas import tpu as pltpu
from jax.sharding import PartitionSpec as P

HIGH = lax.Precision.HIGHEST
MESH = pl.DeviceIdType.MESH
PIECES = 2
STEPS = 2


def schedule(group, tile_rows, bits):
    chain = [(a, k, h) for a in range(tile_rows) for h in range(PIECES) for k in range(STEPS)]
    tree = []
    events = []
    for n, (a, k, h) in enumerate(chain):
        events.append((n, 0, n, 0))
        found = []
        if a == 0 and k == 0:
            found.append(("fixed", 0, 0, a, k, h))
        if a == 0:
            found.append(("fixed", 1, 1 + k, a, k, h))
        for m in range(group):
            found.append(("own", m, 3 + (a * group + m) * STEPS + k, a, k, h))
        for item in found:
            for r in range(len(bits)):
                events.append((n + 1 + r, 1, len(tree), r))
            tree.append(item)
    return chain, tree, sorted(events)


def gather_kernel(row_count, col_count, tile_rows, x_ref, rows_ref, tree_ref, local_sem, zsend, zrecv, tsend, trecv):
    p = lax.axis_index("row")
    q = lax.axis_index("col")
    group = row_count // col_count
    bits = []
    bit = 2
    while bit < row_count:
        bits.append(bit)
        bit *= 2
    bits.append(1)
    chain, tree, events = schedule(group, tile_rows, bits)
    part = x_ref.shape[1] // PIECES

    barrier = pltpu.get_barrier_semaphore()
    for b in bits:
        pl.semaphore_signal(barrier, inc=1, device_id=(p ^ b, q), device_id_type=MESH)

    @pl.when(q > 0)
    def _():
        pl.semaphore_signal(barrier, inc=1, device_id=(p, q - 1), device_id_type=MESH)

    @pl.when(q < col_count - 1)
    def _():
        pl.semaphore_signal(barrier, inc=1, device_id=(p, q + 1), device_id_type=MESH)

    edges = (q > 0).astype(jnp.int32) + (q < col_count - 1).astype(jnp.int32)
    pl.semaphore_wait(barrier, len(bits) + edges)

    def chain_copy(n, way):
        a, k, h = chain[n]
        spot = pl.ds(h * part, part)
        return pltpu.make_async_remote_copy(
            src_ref=rows_ref.at[k, a, spot], dst_ref=rows_ref.at[k, a, spot],
            send_sem=zsend.at[n, (way + 1) // 2], recv_sem=zrecv.at[n],
            device_id=(p, q + way), device_id_type=MESH)

    def tree_copy(t, r):
        kind, source, slot, a, k, h = tree[t]
        spot = pl.ds(h * part, part)
        return pltpu.make_async_remote_copy(
            src_ref=tree_ref.at[slot, spot], dst_ref=tree_ref.at[slot, spot],
            send_sem=tsend.at[t, r], recv_sem=trecv.at[t],
            device_id=(p ^ bits[r], q), device_id_type=MESH)

    def local(src, dst):
        copy = pltpu.make_async_copy(src, dst, local_sem)
        copy.start()
        copy.wait()

    def relative(t):
        kind, source = tree[t][:2]
        return p ^ (source if kind == "fixed" else q + source * col_count)

    def sends(t, r):
        waiting = 0
        for b in bits[r:]:
            waiting |= b
        return (relative(t) & waiting) == 0

    def receives(t, r):
        later = 0
        for b in bits[r + 1:]:
            later |= b
        rel = relative(t)
        return ((rel & bits[r]) != 0) & ((rel & later) == 0)

    def up(k):
        return (q >= k) & (q < col_count - 1)

    def down(k):
        return (q <= k) & (q > 0)

    for k in range(STEPS):
        @pl.when(q == k)
        def _():
            local(x_ref, rows_ref.at[k])

    for when, what, n, r in events:
        if what == 0:
            k = chain[n][1]

            @pl.when(q != k)
            def _():
                chain_copy(n, 1).wait_recv()

            @pl.when(up(k))
            def _():
                chain_copy(n, 1).start()

            @pl.when(down(k))
            def _():
                chain_copy(n, -1).start()
        else:
            kind, source, slot, a, k, h = tree[n]
            spot = pl.ds(h * part, part)
            if r == 0:
                @pl.when(relative(n) == 0)
                def _():
                    local(rows_ref.at[k, a, spot], tree_ref.at[slot, spot])

            @pl.when(sends(n, r))
            def _():
                tree_copy(n, r).start()

            @pl.when(receives(n, r))
            def _():
                tree_copy(n, r).wait_recv()

    for n in range(len(chain)):
        k = chain[n][1]

        @pl.when(up(k))
        def _():
            chain_copy(n, 1).wait_send()

        @pl.when(down(k))
        def _():
            chain_copy(n, -1).wait_send()

    for t in range(len(tree)):
        for r in range(len(bits)):
            @pl.when(sends(t, r))
            def _():
                tree_copy(t, r).wait_send()


def gather(x, row_count, col_count):
    tile_rows, height, width = x.shape
    group = row_count // col_count
    slots = 3 + tile_rows * group * STEPS
    bits = row_count.bit_length() - 1
    chain, tree, _ = schedule(group, tile_rows, [0] * bits)
    anywhere = pl.BlockSpec(memory_space=pl.ANY)
    return pl.pallas_call(
        functools.partial(gather_kernel, row_count, col_count, tile_rows),
        out_shape=(
            jax.ShapeDtypeStruct((STEPS, tile_rows, height, width), jnp.float32),
            jax.ShapeDtypeStruct((slots, height, width), jnp.float32),
        ),
        in_specs=[anywhere],
        out_specs=(anywhere, anywhere),
        scratch_shapes=[
            pltpu.SemaphoreType.DMA,
            pltpu.SemaphoreType.DMA((len(chain), 2)),
            pltpu.SemaphoreType.DMA((len(chain),)),
            pltpu.SemaphoreType.DMA((len(tree), bits)),
            pltpu.SemaphoreType.DMA((len(tree),)),
        ],
        compiler_params=pltpu.CompilerParams(collective_id=0, has_side_effects=True),
    )(x)


def mm(a, b):
    return jnp.matmul(a, b, precision=HIGH)


def factor_block(block):
    lower = jnp.linalg.cholesky(block)
    eye = jnp.eye(block.shape[0], dtype=jnp.float32)
    return lower, lax.linalg.triangular_solve(lower, eye, left_side=True, lower=True)


def factor_and_inverse(block):
    width = block.shape[0]
    if width <= 128:
        return factor_block(block)
    half = width // 2
    l00, i00 = factor_and_inverse(block[:half, :half])
    l10 = mm(block[half:, :half], i00.T)
    l11, i11 = factor_and_inverse(block[half:, half:] - mm(l10, l10.T))
    i10 = -mm(i11, mm(l10, i00))
    zero = jnp.zeros((half, half), jnp.float32)
    return jnp.block([[l00, zero], [l10, l11]]), jnp.block([[i00, zero], [i10, i11]])


def shards(covariance, keep):
    row_count = lax.axis_size("row")
    col_count = lax.axis_size("col")
    row_here = lax.axis_index("row")
    col_here = lax.axis_index("col")
    tile_rows = covariance.shape[0]
    width = covariance.shape[2]
    tile_cols = covariance.shape[3]
    tiles = covariance.reshape(tile_rows, width, tile_cols, width)
    row_ids = jnp.arange(tile_rows) * row_count + row_here
    col_ids = jnp.arange(tile_cols) * col_count + col_here
    live = (keep.reshape(tile_rows, tile_cols) > 0) & (row_ids[:, None] >= col_ids[None, :])
    first = jnp.where(live[:, 0, None, None], covariance[:, 0, :, 0, 0, :], jnp.float32(0.0))
    marks = jnp.broadcast_to(live[:, 0, None, None].astype(jnp.float32), (tile_rows, 8 * PIECES, width))
    rows, tree = gather(jnp.concatenate([first, marks], 1), row_count, col_count)

    row_marks = rows[1, :, width, :1]
    row_tiles = rows[:, :, :width, :]
    cols = tree[3:].reshape(tile_cols, STEPS, -1, width)
    col_marks = cols[:, 1, width, :1]
    col_tiles = cols[:, :, :width, :]
    diag = tree[:3, :width, :]

    def symmetric(block):
        return (block + block.T) * 0.5

    low0, inv0 = factor_and_inverse(symmetric(diag[0]))
    below = mm(diag[1], inv0.T)
    low1, inv1 = factor_and_inverse(symmetric(diag[2] - mm(below, below.T)))

    def panels(first_tiles, second_tiles, marks, ids):
        ids = ids[:, None, None]
        one = mm(first_tiles, inv0.T)
        one = jnp.where(ids > 0, one, jnp.float32(0.0))
        two = second_tiles - mm(one, below.T) * marks[:, :, None]
        two = jnp.where(ids > 1, mm(two, inv1.T), jnp.float32(0.0))
        return one, two

    row_one, row_two = panels(row_tiles[0], row_tiles[1], row_marks, row_ids)
    col_one, col_two = panels(col_tiles[:, 0], col_tiles[:, 1], col_marks, col_ids)
    row_all = jnp.concatenate([row_one, row_two], 2)
    col_all = jnp.concatenate([col_one, col_two], 2)
    product = jnp.einsum("arb,csb->arcs", row_all, col_all, precision=HIGH)
    tiles = jnp.where(live[:, None, :, None], tiles - product, jnp.float32(0.0))
    ids = row_ids[:, None, None]
    done_one = jnp.where(ids == 0, low0[None], row_one)
    done_two = jnp.where(ids == 1, low1[None], row_two)
    column = jnp.where(col_here == 0, done_one, done_two)
    place = (col_ids < STEPS)[None, None, :, None]
    tiles = jnp.where(place, column[:, :, None, :], tiles)
    return tiles.reshape(tile_rows, 1, width, tile_cols, 1, width)


def solution(mesh):
    placed = (P(None, "row", None, None, "col", None), P(None, "row", None, "col"))
    return jax.shard_map(
        shards,
        mesh=mesh,
        in_specs=placed,
        out_specs=P(None, "row", None, None, "col", None),
        check_vma=False,
    )
```

```python
import jax
import jax.numpy as jnp
from jax import lax
from jax.sharding import PartitionSpec as P

HIGH = lax.Precision.HIGHEST


def from_root(block, axis, source):
    block = jnp.where(lax.axis_index(axis) == source, block, jnp.zeros_like(block))
    return lax.psum(block, axis)


def mm(a, b):
    return jnp.matmul(a, b, precision=HIGH)


def factor_block(block):
    lower = jnp.linalg.cholesky(block)
    eye = jnp.eye(block.shape[0], dtype=jnp.float32)
    return lower, lax.linalg.triangular_solve(lower, eye, left_side=True, lower=True)


def factor_and_inverse(block):
    width = block.shape[0]
    if width <= 128:
        return factor_block(block)
    half = width // 2
    l00, i00 = factor_and_inverse(block[:half, :half])
    l10 = mm(block[half:, :half], i00.T)
    l11, i11 = factor_and_inverse(block[half:, half:] - mm(l10, l10.T))
    i10 = -mm(i11, mm(l10, i00))
    zero = jnp.zeros((half, half), jnp.float32)
    return jnp.block([[l00, zero], [l10, l11]]), jnp.block([[i00, zero], [i10, i11]])


def finish(solved, factor, ids, step):
    return jnp.where(
        ids[:, None, None] > step,
        solved,
        jnp.where(ids[:, None, None] == step, factor[None], jnp.float32(0.0)),
    )


def shards(covariance, keep):
    row_count = lax.axis_size("row")
    col_count = lax.axis_size("col")
    row_here = lax.axis_index("row")
    col_here = lax.axis_index("col")
    tile_rows = covariance.shape[0]
    width = covariance.shape[2]
    tile_cols = covariance.shape[3]
    group = row_count // col_count
    tiles = covariance.reshape(tile_rows, width, tile_cols, width)
    row_ids = jnp.arange(tile_rows) * row_count + row_here
    col_ids = jnp.arange(tile_cols) * col_count + col_here
    live = (keep.reshape(tile_rows, tile_cols) > 0) & (row_ids[:, None] >= col_ids[None, :])
    tiles = jnp.where(live[:, None, :, None], tiles, jnp.float32(0.0))

    def spread_rows(block, step):
        return from_root(block, "col", step % col_count)

    def column_tiles(block):
        received = []
        for member in range(group):
            received.append(from_root(block, "row", col_here + member * col_count))
        stacked = jnp.stack(received, 1)
        return stacked.reshape(tile_rows * group, width, width)

    def factor_panel(column_block, step):
        local_diag = column_block[step // row_count]
        diag_tile = from_root(local_diag, "row", step % row_count)
        on_column = col_here == step % col_count
        factor, inverse = factor_and_inverse((diag_tile + diag_tile.T) * 0.5)
        row_panel = finish(mm(column_block, inverse.T), factor, row_ids, step)
        row_panel = jnp.where(on_column, row_panel, jnp.float32(0.0))
        row_panel = spread_rows(row_panel, step)
        col_panel = column_tiles(row_panel)
        return (row_panel, col_panel)

    def apply_update(block, row_panel, col_panel, step):
        product = jnp.einsum("arb,csb->arcs", row_panel, col_panel, precision=lax.Precision.HIGHEST)
        active = live & (row_ids > step)[:, None] & (col_ids > step)[None, :]
        updated = jnp.where(active[:, None, :, None], block - product, block)
        return jnp.where((col_ids == step)[None, None, :, None], row_panel[:, :, None, :], updated)

    first_rows, first_cols = factor_panel(tiles[:, :, 0, :], 0)
    tiles = apply_update(tiles, first_rows, first_cols, 0)
    second_rows, second_cols = factor_panel(tiles[:, :, 0, :], 1)
    tiles = apply_update(tiles, second_rows, second_cols, 1)
    return tiles.reshape(tile_rows, 1, width, tile_cols, 1, width)


def solution(mesh):
    placed = (P(None, "row", None, None, "col", None), P(None, "row", None, "col"))
    return jax.shard_map(
        shards,
        mesh=mesh,
        in_specs=placed,
        out_specs=P(None, "row", None, None, "col", None),
        check_vma=False,
    )
```

```python
import jax
import jax.numpy as jnp
from jax import lax
from jax.sharding import PartitionSpec as P

HIGH = lax.Precision.HIGHEST


def from_root(block, axis, source):
    block = jnp.where(lax.axis_index(axis) == source, block, jnp.zeros_like(block))
    return lax.psum(block, axis)


def mm(a, b):
    return jnp.matmul(a, b, precision=HIGH)


def factor_block(block):
    lower = jnp.linalg.cholesky(block)
    eye = jnp.eye(block.shape[0], dtype=jnp.float32)
    return lower, lax.linalg.triangular_solve(lower, eye, left_side=True, lower=True)


def factor_and_inverse(block):
    width = block.shape[0]
    if width <= 128:
        return factor_block(block)
    half = width // 2
    l00, i00 = factor_and_inverse(block[:half, :half])
    l10 = mm(block[half:, :half], i00.T)
    l11, i11 = factor_and_inverse(block[half:, half:] - mm(l10, l10.T))
    i10 = -mm(i11, mm(l10, i00))
    zero = jnp.zeros((half, half), jnp.float32)
    return jnp.block([[l00, zero], [l10, l11]]), jnp.block([[i00, zero], [i10, i11]])


def shards(covariance, keep):
    row_count = lax.axis_size("row")
    col_count = lax.axis_size("col")
    row_here = lax.axis_index("row")
    col_here = lax.axis_index("col")
    tile_rows = covariance.shape[0]
    width = covariance.shape[2]
    tile_cols = covariance.shape[3]
    group = row_count // col_count
    tiles = covariance.reshape(tile_rows, width, tile_cols, width)
    row_ids = jnp.arange(tile_rows) * row_count + row_here
    col_ids = jnp.arange(tile_cols) * col_count + col_here
    live = (keep.reshape(tile_rows, tile_cols) > 0) & (row_ids[:, None] >= col_ids[None, :])
    tiles = jnp.where(live[:, None, :, None], tiles, jnp.float32(0.0))

    def column_tiles(block):
        received = []
        for member in range(group):
            received.append(from_root(block, "row", col_here + member * col_count))
        stacked = jnp.stack(received, 1)
        return stacked.reshape(tile_rows * group, width, width)

    def symmetric(block):
        return (block + block.T) * 0.5

    marks = jnp.broadcast_to(live[:, 0, None, None].astype(jnp.float32), (tile_rows, 8, width))
    own = jnp.concatenate([tiles[:, :, 0, :], marks], 1)
    spread = lax.all_gather(own, "col")
    first_tiles = spread[0, :, :width]
    second_tiles = spread[1, :, :width]
    second_live = spread[1, :, width, :1]
    ids = row_ids[:, None, None]
    zero = jnp.float32(0.0)

    diag_tile = from_root(first_tiles[0], "row", 0)
    factor, inverse = factor_and_inverse(symmetric(diag_tile))
    row_one = jnp.where(ids > 0, mm(first_tiles, inverse.T), zero)

    local = row_one[0]
    pair = jnp.stack([local, second_tiles[0] - mm(local, local.T)])
    pair = from_root(pair, "row", 1)
    pair, later_one = lax.optimization_barrier((pair, row_one))
    col_one = column_tiles(later_one)
    below = pair[0]
    second_factor, second_inverse = factor_and_inverse(symmetric(pair[1]))
    reduced = second_tiles - mm(row_one, below.T) * second_live[:, :, None]
    row_two = jnp.where(ids > 1, mm(reduced, second_inverse.T), zero)
    later_two, col_one = lax.optimization_barrier((row_two, col_one))
    col_two = column_tiles(later_two)

    active = live[:, None, :, None]
    col_one = jnp.where(col_ids[:, None, None] > 0, col_one, zero)
    col_two = jnp.where(col_ids[:, None, None] > 1, col_two, zero)
    product = jnp.einsum("arb,csb->arcs", row_one, col_one, precision=HIGH)
    tiles = jnp.where(active, tiles - product, zero)
    product = jnp.einsum("arb,csb->arcs", row_two, col_two, precision=HIGH)
    tiles = jnp.where(active, tiles - product, zero)
    done_one = jnp.where(ids == 0, factor[None], row_one)
    done_two = jnp.where(ids == 1, second_factor[None], row_two)
    column = jnp.where(col_here == 0, done_one, done_two)
    tiles = jnp.where((col_ids < 2)[None, None, :, None], column[:, :, None, :], tiles)
    return tiles.reshape(tile_rows, 1, width, tile_cols, 1, width)


def solution(mesh):
    placed = (P(None, "row", None, None, "col", None), P(None, "row", None, "col"))
    return jax.shard_map(
        shards,
        mesh=mesh,
        in_specs=placed,
        out_specs=P(None, "row", None, None, "col", None),
        check_vma=False,
    )
```
